32 devices in a mesh: obl: 8 (over z, y), scn: 4 (over x, core).
Axes of the slice: x: 2, y: 2, z: 4, core: 2. Of those that a mesh axis runs over, the one named last changes fastest.
Arguments:
- factors: bfloat16 [16384, 128], P('scn'), may hold values from -6 to 6
- idiosyncratic: bfloat16 [16384, 16384], P('obl', 'scn'), may hold values from -6 to 6
- loadings: bfloat16 [16384, 128], P('obl'), may hold values from -0.375 to 0.375
- rating: int32 [16384], P('obl'), may hold values from 0 to 15
- barrier: float32 [16], replicated, may hold values from 1 to 3
- loss_given: float32 [16384], P('obl'), may hold values from 0.2 to 0.9
- sector: int32 [16384], P('obl'), may hold values from 0 to 15, as said below
- allowed: int32 [256, 16], replicated, may hold values from 0 to 1, as said below
- holdings: float32 [16384, 256], P('obl'), may hold values from 0.1 to 10
Outputs:
- positions: float32 [16384, 256], P('obl')
- shortfall: float32 [2, 256], replicated
The draws below stay inside these ranges and needn't reach their ends.
Inputs may be any that keep to these rules, and one draw needn't show every extreme that they name: Each sector holds exactly 1024 obligors. `allowed`: every mandate allows at least one sector.
All inputs are finite; a program needn't handle non-finite values.
Results may differ from the reference program's by a relative error of at most 0.0003.
Values may be sent and summed in bfloat16 or wider, within the bound.
A program may use at most 128 MiB of HBM per device.

```python
import math
import jax
import jax.numpy as jnp
from jax import lax

FACTORS = 128
MANDATES = 256
RATINGS = 16
SECTORS = 16
STEPS = 2
OBL_DEV = 2048
OBLIGORS = 16384
SCENARIOS = 16384


def draw_sector(key, part):
    shuffled = jax.random.permutation(key, OBLIGORS)
    return (shuffled % SECTORS).astype(jnp.int32)


def draw_allowed(key, part):
    random_bits = jax.random.randint(jax.random.fold_in(key, 11), (MANDATES, SECTORS), 0, 2)
    chosen = jax.random.randint(jax.random.fold_in(key, 12), (MANDATES,), 0, SECTORS)
    forced = jnp.arange(SECTORS)[None, :] == chosen[:, None]
    return jnp.where(forced, 1, random_bits).astype(jnp.int32)


def touch_ends(result, key, smallest, top_value):
    longest = result.shape.index(max(result.shape))
    spots = []
    for shift in (0, 1):
        where = [jax.random.randint(jax.random.fold_in(key, axis), (), 0, length) for axis, length in enumerate(result.shape)]
        where[longest] = (where[longest] + shift) % result.shape[longest]
        spots.append(tuple(where))
    return result.at[spots[0]].set(smallest).at[spots[1]].set(top_value)


def block_levels(key, extent, shards, low, high):
    def one(dim, blocks):
        draws = jax.random.uniform(jax.random.fold_in(jax.random.fold_in(key, 6), dim), (blocks,), jnp.float32, low / len(shards), high / len(shards))
        return jnp.repeat(jnp.exp(draws), extent[dim] // blocks).reshape((-1,) + (1,) * (len(extent) - dim - 1))

    loudness = one(*shards[0])
    for cut in shards[1:]:
        loudness = loudness * one(*cut)
    return loudness


def scatter_about(key, dims, scale, bound, split=(), kind=jnp.bfloat16):
    values = jax.random.normal(key, dims, jnp.float32) * scale
    if len(split) > 0:
        values = block_levels(key, dims, split, -0.22, 0.18) * values
    return jnp.clip(values, min=-bound, max=bound).astype(kind)


def setup_inputs(seed: int = 0) -> dict:
    streams_of = jax.random.split(jax.random.key(seed), 10)
    factors = scatter_about(streams_of[0], (SCENARIOS, FACTORS), 1.0, 6.0, ((0, 4),))
    idiosyncratic = scatter_about(streams_of[1], (OBLIGORS, SCENARIOS), 1.0, 6.0, ((0, 8), (1, 4)))
    loadings = scatter_about(streams_of[2], (OBLIGORS, FACTORS), (2 * FACTORS) ** -0.5, 0.375, ((0, 8),))
    rating = touch_ends(jax.random.randint(streams_of[3], (OBLIGORS,), 0, RATINGS), jax.random.fold_in(streams_of[3], 1), 0, RATINGS - 1).astype(jnp.int32)
    barrier = jnp.clip(jax.random.uniform(streams_of[4], (RATINGS,), jnp.float32, 1.0, 3.0), 1.0, 3.0)
    loss_given = jnp.clip(0.2 + 0.7 * jax.random.uniform(streams_of[5], (OBLIGORS,), jnp.float32) ** block_levels(streams_of[5], (OBLIGORS,), ((0, 8),), -0.2, 0.2), 0.2, 0.9)
    sector = draw_sector(jax.random.fold_in(streams_of[9], 71), 0)
    allowed = draw_allowed(jax.random.fold_in(streams_of[9], 71), 0)
    holdings = jnp.clip(jnp.exp(math.log(10.0) - 4.6051702 * jax.random.uniform(streams_of[8], (OBLIGORS, MANDATES), jnp.float32) ** block_levels(streams_of[8], (OBLIGORS, MANDATES), ((0, 8),), -0.2, 0.2)), 0.1, 10.0)
    return {"factors": factors, "idiosyncratic": idiosyncratic, "loadings": loadings, "rating": rating, "barrier": barrier, "loss_given": loss_given, "sector": sector, "allowed": allowed, "holdings": holdings}


IDIO_SCALE = 0.8
SHARP = 2.0
LEVEL = 0.99
QUANTILE = 2.326
SMOOTH = 0.5
EPSILON = 1e-06
STEP_RATE = 8.0

def default_block(load_rows, idio_rows, barrier_rows, factors):
    systematic = lax.dot_general(load_rows, factors, (((1,), (1,)), ((), ())), preferred_element_type=jnp.float32)
    latent = systematic + IDIO_SCALE * idio_rows.astype(jnp.float32)
    return jax.nn.sigmoid((latent - barrier_rows[:, None]) * SHARP).astype(jnp.bfloat16)

def reference(factors, idiosyncratic, loadings, rating, barrier, loss_given, sector, allowed, holdings):
    eligible = jnp.transpose(allowed)[sector].astype(jnp.float32)
    barrier_rows = barrier[rating]
    blocks = OBLIGORS // OBL_DEV
    load_blocks = loadings.reshape(blocks, OBL_DEV, FACTORS)
    idio_blocks = idiosyncratic.reshape(blocks, OBL_DEV, SCENARIOS)
    bar_blocks = barrier_rows.reshape(blocks, OBL_DEV)
    weighted = eligible * holdings
    positions = OBLIGORS * weighted / lax.optimization_barrier(jnp.sum(weighted, 0))
    tail_scale = 1.0 / ((1.0 - LEVEL) * SCENARIOS)
    results = []
    for iteration in range(STEPS):
        exposure = (loss_given[:, None] * positions / OBLIGORS).astype(jnp.bfloat16)
        expo_blocks = exposure.reshape(blocks, OBL_DEV, MANDATES)

        def accumulate(carry, pieces):
            default_prob = default_block(pieces[0], pieces[1], pieces[2], factors)
            term = lax.dot_general(default_prob, pieces[3], (((0,), (0,)), ((), ())), preferred_element_type=jnp.float32)
            return (carry + term, None)
        losses, unused = lax.scan(accumulate, jnp.zeros((SCENARIOS, MANDATES), jnp.float32), (load_blocks, idio_blocks, bar_blocks, expo_blocks))
        center = lax.optimization_barrier(jnp.sum(losses, 0)) / SCENARIOS
        deviate = losses - center
        spread = lax.optimization_barrier(jnp.sum(deviate * deviate, 0)) / SCENARIOS
        deviation = jnp.sqrt(spread + EPSILON)
        thresh = center + QUANTILE * deviation
        smooth_width = SMOOTH * deviation
        scaled = (losses - thresh) / smooth_width
        tail_weight = (jax.nn.sigmoid(scaled) * tail_scale).astype(jnp.bfloat16)
        tail_sum = lax.optimization_barrier(jnp.sum(jax.nn.softplus(scaled), 0))
        results.append(thresh + smooth_width * (tail_sum * tail_scale))

        def project(pieces):
            default_prob = default_block(pieces[0], pieces[1], pieces[2], factors)
            return jnp.dot(default_prob, tail_weight, preferred_element_type=jnp.float32)
        gradient = lax.map(project, (load_blocks, idio_blocks, bar_blocks)).reshape(OBLIGORS, MANDATES)
        gradient = loss_given[:, None] * eligible * gradient
        unnorm = positions * jnp.exp(-STEP_RATE * gradient)
        positions = OBLIGORS * unnorm / lax.optimization_barrier(jnp.sum(unnorm, 0))
    return (positions, jnp.stack(results))
```

```python
import functools

import jax
import jax.numpy as jnp
from jax import lax
from jax.experimental import pallas as pl
from jax.experimental.pallas import tpu as pltpu
from jax.sharding import PartitionSpec as P

STEPS = 2


IDIO_SCALE = 0.8
SHARP = 2.0
LEVEL = 0.99
QUANTILE = 2.326
SMOOTH = 0.5
EPSILON = 1e-06
STEP_RATE = 8.0

MESH = pl.DeviceIdType.MESH
VMEM = pl.BlockSpec(memory_space=pltpu.VMEM)
LIMIT = 48 * 1024 * 1024
F32 = jnp.float32
BF16 = jnp.bfloat16


def push(src, dst, send, recv, axis, peer):
    return pltpu.make_async_remote_copy(
        src_ref=src,
        dst_ref=dst,
        send_sem=send,
        recv_sem=recv,
        device_id={axis: peer},
        device_id_type=MESH,
    )


def greet(groups):
    barrier = pltpu.get_barrier_semaphore()
    total = 0
    for axis, rank, size in groups:
        for step in range(1, size):
            pl.semaphore_signal(
                barrier, inc=1, device_id={axis: lax.rem(rank + step, size)}, device_id_type=MESH
            )
        total += size - 1
    pl.semaphore_wait(barrier, total)


def spread_out(buf, send, recv, axis, rank, size):
    copies = []
    for step in range(1, size):
        copy = push(
            buf.at[rank], buf.at[rank], send.at[step - 1], recv.at[step - 1], axis, lax.rem(rank + step, size)
        )
        copy.start()
        copies.append(copy)
    return copies


def wait_all(copies):
    for copy in copies:
        copy.wait()


def total_kernel(n, x_ref, o_ref, buf, send, recv):
    rank = lax.axis_index("obl")
    greet([("obl", rank, n)])
    buf[rank] = x_ref[...]
    wait_all(spread_out(buf, send, recv, "obl", rank, n))
    o_ref[...] = jnp.sum(buf[...], axis=0)


def total_over_obl(value, n):
    return pl.pallas_call(
        functools.partial(total_kernel, n),
        out_shape=jax.ShapeDtypeStruct(value.shape, F32),
        in_specs=[VMEM],
        out_specs=VMEM,
        scratch_shapes=[
            pltpu.VMEM((n,) + value.shape, F32),
            pltpu.SemaphoreType.DMA((n - 1,)),
            pltpu.SemaphoreType.DMA((n - 1,)),
        ],
        compiler_params=pltpu.CompilerParams(collective_id=0, has_side_effects=True),
    )(value)


def tail_kernel(
    n, ns, scenarios, tail_scale,
    part_ref, w_ref, short_ref,
    away, near, far_out, far_in, losses,
    off_buf, sum_buf, scn_buf, tail_buf, tail_scn,
    off_s, off_r, sum_s, sum_r, scn_s, scn_r, tail_s, tail_r, ts_s, ts_r,
    a_s, a_r, b_s, b_r, c_s, c_r, d_s, d_r,
):
    obl = lax.axis_index("obl")
    scn = lax.axis_index("scn")
    outer, inner = obl // 2, lax.rem(obl, 2)
    nz = n // 2
    mate = outer * 2 + 1 - inner
    rows, cols = part_ref.shape[1:]
    local = n * rows
    targets = [lax.rem(outer + 1 + i, nz) for i in range(nz)]

    greet([("obl", obl, n), ("scn", scn, ns)])
    offset = jnp.sum(part_ref[0], axis=0, keepdims=True) * (1.0 / rows)
    off_buf[obl] = jnp.broadcast_to(offset, (8, cols))
    pair = []
    for i in range(nz):
        away[i] = (part_ref[targets[i] * 2 + 1 - inner] - offset).astype(BF16)
        copy = push(away.at[i], near.at[i], a_s.at[i], a_r.at[i], "obl", mate)
        copy.start()
        pair.append(copy)
    offsets = spread_out(off_buf, off_s, off_r, "obl", obl, n)
    line = []
    for i in range(nz - 1):
        mine = part_ref[targets[i] * 2 + inner] - offset
        pair[i].wait_recv()
        far_out[i] = (mine + near[i].astype(F32)).astype(BF16)
        copy = push(far_out.at[i], far_in.at[i], b_s.at[i], b_r.at[i], "obl", targets[i] * 2 + inner)
        copy.start()
        line.append(copy)
    pair[nz - 1].wait_recv()
    losses[...] = (part_ref[obl] - offset) + near[nz - 1].astype(F32)
    for i in range(nz - 1):
        line[i].wait_recv()
        losses[...] += far_in[i].astype(F32)
    value = losses[...]
    first = jnp.sum(value, axis=0, keepdims=True)
    second = jnp.sum(value * value, axis=0, keepdims=True)
    row = lax.broadcasted_iota(jnp.int32, (8, cols), 0)
    sum_buf[obl] = jnp.where(row == 0, first, second)
    wait_all(offsets)
    wait_all(spread_out(sum_buf, sum_s, sum_r, "obl", obl, n))
    base = jnp.sum(off_buf[...], axis=0)
    scn_buf[scn] = jnp.where(row == 2, base, jnp.sum(sum_buf[...], axis=0))
    wait_all(spread_out(scn_buf, scn_s, scn_r, "scn", scn, ns))
    center = jnp.zeros((1, cols), F32)
    for k in range(ns):
        center += scn_buf[k, 0:1, :] + local * scn_buf[k, 2:3, :]
    center = center / scenarios
    spread = jnp.zeros((1, cols), F32)
    for k in range(ns):
        gap = scn_buf[k, 2:3, :] - center
        spread += scn_buf[k, 1:2, :] + 2.0 * gap * scn_buf[k, 0:1, :] + local * (gap * gap)
    spread = spread / scenarios
    deviation = jnp.sqrt(spread + EPSILON)
    thresh = center + QUANTILE * deviation
    width = SMOOTH * deviation
    shift = base[0:1, :] - thresh
    scaled = (losses[...] + shift) / width
    w_ref[obl] = (jax.nn.sigmoid(scaled) * tail_scale).astype(BF16)

    gather = []
    own = push(w_ref.at[obl], w_ref.at[obl], d_s.at[nz - 1], d_r.at[nz - 1], "obl", mate)
    own.start()
    for i in range(nz - 1):
        copy = push(w_ref.at[obl], w_ref.at[obl], c_s.at[i], c_r.at[i], "obl", targets[i] * 2 + inner)
        copy.start()
        gather.append(copy)
    soft = jnp.maximum(scaled, 0.0) + jnp.log1p(jnp.exp(-jnp.abs(scaled)))
    tail_buf[obl] = jnp.broadcast_to(jnp.sum(soft, axis=0, keepdims=True), (8, cols))
    tails = spread_out(tail_buf, tail_s, tail_r, "obl", obl, n)
    passed = [own]
    for i in range(nz - 1):
        gather[i].wait_recv()
        slot = lax.rem(outer + nz - 1 - i, nz) * 2 + inner
        copy = push(w_ref.at[slot], w_ref.at[slot], d_s.at[i], d_r.at[i], "obl", mate)
        copy.start()
        passed.append(copy)
    wait_all(tails)
    tail_scn[scn] = jnp.sum(tail_buf[...], axis=0)
    wait_all(spread_out(tail_scn, ts_s, ts_r, "scn", scn, ns))
    tail_sum = jnp.sum(tail_scn[...], axis=0)
    short_ref[...] = thresh + width * (tail_sum * tail_scale)
    for copy in pair + line + gather:
        copy.wait_send()
    wait_all(passed)


def tail_weights(partial, n, ns, scenarios, tail_scale):
    local, cols = partial.shape
    rows = local // n
    nz = n // 2
    dma = pltpu.SemaphoreType.DMA
    weights, short = pl.pallas_call(
        functools.partial(tail_kernel, n, ns, scenarios, tail_scale),
        out_shape=(
            jax.ShapeDtypeStruct((n, rows, cols), BF16),
            jax.ShapeDtypeStruct((8, cols), F32),
        ),
        in_specs=[VMEM],
        out_specs=(VMEM, VMEM),
        scratch_shapes=[
            pltpu.VMEM((nz, rows, cols), BF16),
            pltpu.VMEM((nz, rows, cols), BF16),
            pltpu.VMEM((nz - 1, rows, cols), BF16),
            pltpu.VMEM((nz - 1, rows, cols), BF16),
            pltpu.VMEM((rows, cols), F32),
            pltpu.VMEM((n, 8, cols), F32),
            pltpu.VMEM((n, 8, cols), F32),
            pltpu.VMEM((ns, 8, cols), F32),
            pltpu.VMEM((n, 8, cols), F32),
            pltpu.VMEM((ns, 8, cols), F32),
        ]
        + [dma((n - 1,))] * 4
        + [dma((ns - 1,))] * 2
        + [dma((n - 1,))] * 2
        + [dma((ns - 1,))] * 2
        + [dma((nz,))] * 2
        + [dma((nz - 1,))] * 4
        + [dma((nz,))] * 2,
        compiler_params=pltpu.CompilerParams(
            collective_id=1, has_side_effects=True, vmem_limit_bytes=LIMIT
        ),
    )(partial.reshape(n, rows, cols))
    return weights.reshape(local, cols), short


def update_kernel(
    n, ns, obligors, last,
    grad_ref, pos_ref, elig_ref, given_ref, new_ref, out_ref,
    near, far_out, far_in, scn_buf, obl_buf,
    scn_s, scn_r, obl_s, obl_r,
    a_s, a_r, b_s, b_r, c_s, c_r, d_s, d_r,
):
    obl = lax.axis_index("obl")
    scn = lax.axis_index("scn")
    outer, inner = scn // 2, lax.rem(scn, 2)
    nx = ns // 2
    mate = outer * 2 + 1 - inner
    rows, cols = grad_ref.shape[1:]
    targets = [lax.rem(outer + 1 + i, nx) for i in range(nx)]

    greet([("obl", obl, n), ("scn", scn, ns)])
    pair = []
    for i in range(nx):
        slot = targets[i] * 2 + 1 - inner
        copy = push(grad_ref.at[slot], near.at[i], a_s.at[i], a_r.at[i], "scn", mate)
        copy.start()
        pair.append(copy)
    line = []
    for i in range(nx - 1):
        slot = targets[i] * 2 + inner
        pair[i].wait_recv()
        far_out[i] = grad_ref[slot] + near[i]
        copy = push(far_out.at[i], far_in.at[i], b_s.at[i], b_r.at[i], "scn", slot)
        copy.start()
        line.append(copy)
    pair[nx - 1].wait_recv()
    gradient = grad_ref[scn] + near[nx - 1]
    for i in range(nx - 1):
        line[i].wait_recv()
        gradient += far_in[i]
    gradient = given_ref[...] * elig_ref[...] * gradient
    unnorm = pos_ref[...] * jnp.exp(-STEP_RATE * gradient)
    new_ref[...] = unnorm
    scn_buf[scn] = jnp.broadcast_to(jnp.sum(unnorm, axis=0, keepdims=True), (8, cols))
    wait_all(spread_out(scn_buf, scn_s, scn_r, "scn", scn, ns))
    obl_buf[obl] = jnp.sum(scn_buf[...], axis=0)
    wait_all(spread_out(obl_buf, obl_s, obl_r, "obl", obl, n))
    total = jnp.sum(obl_buf[...], axis=0)[0:1, :]
    new = obligors * new_ref[...] / total
    new_ref[...] = new
    if last:
        out_ref[scn] = new
    else:
        out_ref[scn] = (given_ref[...] * new / obligors).astype(BF16)
    own = push(out_ref.at[scn], out_ref.at[scn], d_s.at[nx - 1], d_r.at[nx - 1], "scn", mate)
    own.start()
    gather = []
    for i in range(nx - 1):
        copy = push(out_ref.at[scn], out_ref.at[scn], c_s.at[i], c_r.at[i], "scn", targets[i] * 2 + inner)
        copy.start()
        gather.append(copy)
    passed = [own]
    for i in range(nx - 1):
        gather[i].wait_recv()
        slot = lax.rem(outer + nx - 1 - i, nx) * 2 + inner
        copy = push(out_ref.at[slot], out_ref.at[slot], d_s.at[i], d_r.at[i], "scn", mate)
        copy.start()
        passed.append(copy)
    for copy in pair + line + gather:
        copy.wait_send()
    wait_all(passed)


def update(gradient, positions, eligible, given, n, ns, obligors, last):
    local, cols = gradient.shape
    rows = local // ns
    nx = ns // 2
    dma = pltpu.SemaphoreType.DMA
    new, out = pl.pallas_call(
        functools.partial(update_kernel, n, ns, obligors, last),
        out_shape=(
            jax.ShapeDtypeStruct((rows, cols), F32),
            jax.ShapeDtypeStruct((ns, rows, cols), F32 if last else BF16),
        ),
        in_specs=[VMEM] * 4,
        out_specs=(VMEM, VMEM),
        scratch_shapes=[
            pltpu.VMEM((nx, rows, cols), F32),
            pltpu.VMEM((nx - 1, rows, cols), F32),
            pltpu.VMEM((nx - 1, rows, cols), F32),
            pltpu.VMEM((ns, 8, cols), F32),
            pltpu.VMEM((n, 8, cols), F32),
        ]
        + [dma((ns - 1,))] * 2
        + [dma((n - 1,))] * 2
        + [dma((nx,))] * 2
        + [dma((nx - 1,))] * 4
        + [dma((nx,))] * 2,
        compiler_params=pltpu.CompilerParams(
            collective_id=3 if last else 2, has_side_effects=True, vmem_limit_bytes=LIMIT
        ),
    )(gradient.reshape(ns, rows, cols), positions, eligible, given)
    return new, out.reshape(local, cols)


def on_device(
    factors, idiosyncratic, loadings, rating, barrier, loss_given, sector, allowed, holdings
):
    obl_dev = idiosyncratic.shape[0]
    scn_dev = idiosyncratic.shape[1]
    n = lax.axis_size("obl")
    ns = lax.axis_size("scn")
    obligors = obl_dev * n
    scenarios = scn_dev * ns
    tail_scale = 1.0 / ((1.0 - LEVEL) * scenarios)
    sector_hot = (sector[:, None] == jnp.arange(allowed.shape[1])[None, :]).astype(jnp.float32)
    eligible = lax.dot_general(
        sector_hot,
        allowed.astype(jnp.float32),
        (((1,), (1,)), ((), ())),
        precision=lax.Precision.HIGHEST,
    )
    rating_hot = (rating[:, None] == jnp.arange(barrier.shape[0])[None, :]).astype(jnp.float32)
    barrier_rows = jnp.dot(rating_hot, barrier, precision=lax.Precision.HIGHEST)
    weighted = eligible * holdings
    local_total = jnp.broadcast_to(jnp.sum(weighted, 0)[None, :], (8, weighted.shape[1]))
    totals = total_over_obl(local_total, n)[0]
    positions = obligors * weighted / totals
    systematic = lax.dot_general(
        loadings, factors, (((1,), (1,)), ((), ())), preferred_element_type=jnp.float32
    )
    latent = systematic + IDIO_SCALE * idiosyncratic.astype(jnp.float32)
    default_prob = jax.nn.sigmoid((latent - barrier_rows[:, None]) * SHARP).astype(jnp.bfloat16)
    exposure = (loss_given[:, None] * positions / obligors).astype(jnp.bfloat16)
    part = obl_dev // ns
    begin = lax.axis_index("scn") * part
    shard = lax.dynamic_slice_in_dim(positions, begin, part, 0)
    eligible_shard = lax.dynamic_slice_in_dim(eligible, begin, part, 0)
    given_shard = lax.dynamic_slice_in_dim(loss_given, begin, part, 0)[:, None]
    results = []
    for iteration in range(STEPS):
        last = iteration == STEPS - 1
        partial_value = lax.dot_general(
            default_prob, exposure, (((0,), (0,)), ((), ())), preferred_element_type=jnp.float32
        )
        tail_weight, short = tail_weights(partial_value, n, ns, scenarios, tail_scale)
        results.append(short[0])
        gradient = jnp.dot(default_prob, tail_weight, preferred_element_type=jnp.float32)
        shard, out = update(gradient, shard, eligible_shard, given_shard, n, ns, obligors, last)
        exposure = out
    return (out, jnp.stack(results))


def solution(mesh):
    return jax.shard_map(
        on_device,
        mesh=mesh,
        in_specs=(
            P("scn", None),
            P("obl", "scn"),
            P("obl", None),
            P("obl"),
            P(),
            P("obl"),
            P("obl"),
            P(),
            P("obl", None),
        ),
        out_specs=(P("obl", None), P()),
        check_vma=False,
    )
```

```python
import functools

import jax
import jax.numpy as jnp
from jax import lax
from jax.experimental import pallas as pl
from jax.experimental.pallas import tpu as pltpu
from jax.sharding import PartitionSpec as P

STEPS = 2


IDIO_SCALE = 0.8
SHARP = 2.0
LEVEL = 0.99
QUANTILE = 2.326
SMOOTH = 0.5
EPSILON = 1e-06
STEP_RATE = 8.0

MESH = pl.DeviceIdType.MESH
VMEM = pl.BlockSpec(memory_space=pltpu.VMEM)
LIMIT = 60 * 1024 * 1024
F32 = jnp.float32
BF16 = jnp.bfloat16


def push(src, dst, send, recv, axis, peer):
    return pltpu.make_async_remote_copy(
        src_ref=src,
        dst_ref=dst,
        send_sem=send,
        recv_sem=recv,
        device_id={axis: peer},
        device_id_type=MESH,
    )


def greet(groups):
    barrier = pltpu.get_barrier_semaphore()
    total = 0
    for axis, rank, size in groups:
        for step in range(1, size):
            pl.semaphore_signal(
                barrier, inc=1, device_id={axis: lax.rem(rank + step, size)}, device_id_type=MESH
            )
        total += size - 1
    pl.semaphore_wait(barrier, total)


def spread_out(buf, send, recv, axis, rank, size):
    copies = []
    for step in range(1, size):
        copy = push(
            buf.at[rank], buf.at[rank], send.at[step - 1], recv.at[step - 1], axis, lax.rem(rank + step, size)
        )
        copy.start()
        copies.append(copy)
    return copies


def wait_all(copies):
    for copy in copies:
        copy.wait()


def kernel(
    n, ns, obligors, scenarios, tail_scale,
    idio_ref, fact_ref, load_ref, bar_ref, given_ref, elig_ref, hold_ref,
    out_ref, short_ref,
    prob, expo, acc, away, near, far_out, far_in, losses, weight,
    grad, grad_near, grad_out, grad_in, pos,
    tot_buf, off_buf, sum_buf, scn_buf, tail_buf, tail_scn, new_scn, new_obl,
    load_sem, tot_sem,
    off_sem, sum_sem, scn_sem, tail_sem, tsc_sem, nsc_sem, nob_sem,
    a_sem, b_sem, c_sem, d_sem, ga_sem, gb_sem, gc_sem, gd_sem,
):
    obl = lax.axis_index("obl")
    scn = lax.axis_index("scn")
    outer, inner = obl // 2, lax.rem(obl, 2)
    nz = n // 2
    mate = outer * 2 + 1 - inner
    souter, sinner = scn // 2, lax.rem(scn, 2)
    nx = ns // 2
    smate = souter * 2 + 1 - sinner
    obl_dev, cols = hold_ref.shape
    scn_dev = fact_ref.shape[0]
    rows = scn_dev // n
    part = obl_dev // ns
    targets = [lax.rem(outer + 1 + i, nz) for i in range(nz)]
    mates = [t * 2 + 1 - inner for t in targets]
    owns = [t * 2 + inner for t in targets]
    stargets = [lax.rem(souter + 1 + i, nx) for i in range(nx)]
    order = [p for pair in zip(mates, owns) for p in pair]

    loads = {}
    for where, piece in enumerate(order):
        copy = pltpu.make_async_copy(
            idio_ref.at[:, pl.ds(pl.multiple_of(piece * rows, 128), rows)], prob.at[piece], load_sem.at[where]
        )
        copy.start()
        loads[where] = copy
    total = jnp.zeros((1, cols), F32)
    for k in range(ns):
        span = pl.ds(k * part, part)
        total += jnp.sum(elig_ref[span, :] * hold_ref[span, :], axis=0, keepdims=True)
    tot_buf[obl] = jnp.broadcast_to(total, (8, cols))
    greet([("obl", obl, n), ("scn", scn, ns)])
    totals = spread_out(tot_buf, tot_sem.at[0], tot_sem.at[1], "obl", obl, n)
    tile = min(256, part)

    def probabilities(where):
        piece = order[where]
        loads[where].wait()
        fact = fact_ref[pl.ds(pl.multiple_of(piece * rows, 128), rows), :]

        @pl.loop(0, obl_dev // tile)
        def _(t):
            span = pl.ds(pl.multiple_of(t * tile, tile), tile)
            latent = lax.dot_general(
                load_ref[span, :], fact, (((1,), (1,)), ((), ())), preferred_element_type=F32
            )
            latent = latent + IDIO_SCALE * prob[piece, span, :].astype(F32)
            prob[piece, span, :] = jax.nn.sigmoid((latent - bar_ref[span, :]) * SHARP).astype(BF16)

    def partial_losses(step, piece):
        acc[...] = jnp.zeros_like(acc)

        @pl.loop(0, ns)
        def _(k):
            span = pl.ds(pl.multiple_of(k * part, part), part)
            acc[...] += jnp.dot(expo[step, k], prob[piece, span, :], preferred_element_type=F32)

    def add_gradient(piece, k, weights, fresh):
        span = pl.ds(pl.multiple_of(k * part, part), part)
        value = jnp.dot(prob[piece, span, :], weights, preferred_element_type=F32)
        if fresh:
            grad[k] = value
        else:
            grad[k] += value

    def add_piece(step, piece, fresh=False):
        weights = weight[step, piece]

        @pl.loop(0, ns)
        def _(k):
            add_gradient(piece, k, weights, fresh)

    probabilities(0)
    wait_all(totals)
    total = jnp.sum(tot_buf[...], axis=0)[0:1, :]
    for k in range(ns):
        span = pl.ds(k * part, part)
        start = obligors * (elig_ref[span, :] * hold_ref[span, :]) / total
        expo[0, k] = jnp.transpose(given_ref[span, :] * start / obligors).astype(BF16)
    mine = pl.ds(pl.multiple_of(scn * part, part), part)
    pos[...] = obligors * (elig_ref[mine, :] * hold_ref[mine, :]) / total
    row = lax.broadcasted_iota(jnp.int32, (8, cols), 0)

    for step in range(STEPS):
        last = step == STEPS - 1
        pair, line = [], []
        offset = None

        def send_mate(i):
            nonlocal offset
            if step == 0 and i > 0:
                probabilities(2 * i)
            partial_losses(step, mates[i])
            if i == 0:
                offset = jnp.sum(acc[...], axis=1, keepdims=True) * (1.0 / rows)
                off_buf[step, obl] = jnp.transpose(jnp.broadcast_to(offset, (cols, 128)))[0:8, :]
            away[i] = (acc[...] - offset).astype(BF16)
            copy = push(away.at[i], near.at[step, i], a_sem.at[step, 0, i], a_sem.at[step, 1, i], "obl", mate)
            copy.start()
            pair.append(copy)

        send_mate(0)
        offsets = spread_out(off_buf.at[step], off_sem.at[step, 0], off_sem.at[step, 1], "obl", obl, n)
        send_mate(1)
        for i in range(nz):
            if step == 0:
                probabilities(2 * i + 1)
            partial_losses(step, owns[i])
            pair[i].wait_recv()
            value = acc[...] - offset + near[step, i].astype(F32)
            if i < nz - 1:
                far_out[i] = value.astype(BF16)
                copy = push(
                    far_out.at[i], far_in.at[step, i], b_sem.at[step, 0, i], b_sem.at[step, 1, i], "obl", owns[i]
                )
                copy.start()
                line.append(copy)
            else:
                losses[...] = value
            if i + 2 < nz:
                send_mate(i + 2)
        wait_all(offsets)
        for i in range(nz - 1):
            line[i].wait_recv()
            losses[...] += far_in[step, i].astype(F32)
        value = jnp.transpose(losses[...])
        first = jnp.sum(value, axis=0, keepdims=True)
        second = jnp.sum(value * value, axis=0, keepdims=True)
        sum_buf[step, obl] = jnp.where(row == 0, first, second)
        wait_all(spread_out(sum_buf.at[step], sum_sem.at[step, 0], sum_sem.at[step, 1], "obl", obl, n))
        base = jnp.sum(off_buf[step], axis=0)
        scn_buf[step, scn] = jnp.where(row == 2, base, jnp.sum(sum_buf[step], axis=0))
        wait_all(spread_out(scn_buf.at[step], scn_sem.at[step, 0], scn_sem.at[step, 1], "scn", scn, ns))
        center = jnp.zeros((1, cols), F32)
        for k in range(ns):
            center += scn_buf[step, k, 0:1, :] + scn_dev * scn_buf[step, k, 2:3, :]
        center = center / scenarios
        spread = jnp.zeros((1, cols), F32)
        for k in range(ns):
            gap = scn_buf[step, k, 2:3, :] - center
            spread += scn_buf[step, k, 1:2, :] + 2.0 * gap * scn_buf[step, k, 0:1, :] + scn_dev * (gap * gap)
        spread = spread / scenarios
        deviation = jnp.sqrt(spread + EPSILON)
        thresh = center + QUANTILE * deviation
        width = SMOOTH * deviation
        scaled = (jnp.transpose(losses[...]) + (base[0:1, :] - thresh)) / width
        weight[step, obl] = (jax.nn.sigmoid(scaled) * tail_scale).astype(BF16)

        def give(slot, index, sems, axis, peer):
            ref = weight.at[step, slot]
            copy = push(ref, ref, sems.at[step, 0, index], sems.at[step, 1, index], axis, peer)
            copy.start()
            return copy

        own = give(obl, nz - 1, d_sem, "obl", mate)
        gather = [give(obl, i, c_sem, "obl", owns[i]) for i in range(nz - 1)]
        soft = jnp.maximum(scaled, 0.0) + jnp.log1p(jnp.exp(-jnp.abs(scaled)))
        tail_buf[step, obl] = jnp.broadcast_to(jnp.sum(soft, axis=0, keepdims=True), (8, cols))
        tails = spread_out(tail_buf.at[step], tail_sem.at[step, 0], tail_sem.at[step, 1], "obl", obl, n)
        add_piece(step, obl, fresh=True)
        own.wait_recv()
        add_piece(step, mate)
        passed = []
        sources = [lax.rem(outer + nz - 1 - i, nz) for i in range(nz - 1)]
        for i in range(nz - 1):
            gather[i].wait_recv()
            slot = sources[i] * 2 + inner
            passed.append(give(slot, i, d_sem, "obl", mate))
            add_piece(step, slot)
        wait_all(tails)
        tail_scn[step, scn] = jnp.sum(tail_buf[step], axis=0)
        scn_tails = spread_out(tail_scn.at[step], tsc_sem.at[step, 0], tsc_sem.at[step, 1], "scn", scn, ns)
        for i in range(nz - 2):
            passed[i].wait_recv()
            add_piece(step, sources[i] * 2 + 1 - inner)
        passed[nz - 2].wait_recv()
        final = sources[nz - 2] * 2 + 1 - inner
        final_weights = weight[step, final]

        gpair, gline = [], []
        for i in range(nx):
            slot = stargets[i] * 2 + 1 - sinner
            add_gradient(final, slot, final_weights, False)
            copy = push(
                grad.at[slot], grad_near.at[step, i], ga_sem.at[step, 0, i], ga_sem.at[step, 1, i], "scn", smate
            )
            copy.start()
            gpair.append(copy)
        for i in range(nx):
            slot = stargets[i] * 2 + sinner
            add_gradient(final, slot, final_weights, False)
            gpair[i].wait_recv()
            if i < nx - 1:
                grad_out[i] = grad[slot] + grad_near[step, i]
                copy = push(
                    grad_out.at[i], grad_in.at[step, i], gb_sem.at[step, 0, i], gb_sem.at[step, 1, i], "scn", slot
                )
                copy.start()
                gline.append(copy)
        wait_all(scn_tails)
        short_ref[step] = thresh + width * (jnp.sum(tail_scn[step], axis=0) * tail_scale)
        gradient = grad[scn] + grad_near[step, nx - 1]
        for i in range(nx - 1):
            gline[i].wait_recv()
            gradient += grad_in[step, i]
        gradient = given_ref[mine, :] * elig_ref[mine, :] * gradient
        unnorm = pos[...] * jnp.exp(-STEP_RATE * gradient)
        pos[...] = unnorm
        new_scn[step, scn] = jnp.broadcast_to(jnp.sum(unnorm, axis=0, keepdims=True), (8, cols))
        wait_all(spread_out(new_scn.at[step], nsc_sem.at[step, 0], nsc_sem.at[step, 1], "scn", scn, ns))
        new_obl[step, obl] = jnp.sum(new_scn[step], axis=0)
        wait_all(spread_out(new_obl.at[step], nob_sem.at[step, 0], nob_sem.at[step, 1], "obl", obl, n))
        total = jnp.sum(new_obl[step], axis=0)[0:1, :]
        new = obligors * pos[...] / total
        if last:
            out_ref[scn] = new
        else:
            pos[...] = new
            expo[step + 1, scn] = jnp.transpose(given_ref[mine, :] * new / obligors).astype(BF16)

        def hand(slot, index, sems, peer):
            ref = out_ref.at[slot] if last else expo.at[step + 1, slot]
            copy = push(ref, ref, sems.at[step, 0, index], sems.at[step, 1, index], "scn", peer)
            copy.start()
            return copy

        mine_copy = hand(scn, nx - 1, gd_sem, smate)
        ggather = [hand(scn, i, gc_sem, stargets[i] * 2 + sinner) for i in range(nx - 1)]
        gpassed = [mine_copy]
        for i in range(nx - 1):
            ggather[i].wait_recv()
            slot = lax.rem(souter + nx - 1 - i, nx) * 2 + sinner
            gpassed.append(hand(slot, i, gd_sem, smate))
        own.wait_send()
        for copy in pair + line + gather + passed + gpair + gline + ggather:
            copy.wait_send()
        wait_all(gpassed)


def descend(idiosyncratic, factors, loadings, bars, given, eligible, holdings, n, ns, obligors, scenarios, tail_scale):
    obl_dev, cols = holdings.shape
    scn_dev = factors.shape[0]
    rows, part = scn_dev // n, obl_dev // ns
    nz, nx = n // 2, ns // 2
    dma = pltpu.SemaphoreType.DMA
    return pl.pallas_call(
        functools.partial(kernel, n, ns, obligors, scenarios, tail_scale),
        out_shape=(
            jax.ShapeDtypeStruct((ns, part, cols), F32),
            jax.ShapeDtypeStruct((STEPS, 8, cols), F32),
        ),
        in_specs=[pl.BlockSpec(memory_space=pl.ANY)] + [VMEM] * 6,
        out_specs=(VMEM, VMEM),
        scratch_shapes=[
            pltpu.VMEM((n, obl_dev, rows), BF16),
            pltpu.VMEM((STEPS, ns, cols, part), BF16),
            pltpu.VMEM((cols, rows), F32),
            pltpu.VMEM((nz, cols, rows), BF16),
            pltpu.VMEM((STEPS, nz, cols, rows), BF16),
            pltpu.VMEM((nz - 1, cols, rows), BF16),
            pltpu.VMEM((STEPS, nz - 1, cols, rows), BF16),
            pltpu.VMEM((cols, rows), F32),
            pltpu.VMEM((STEPS, n, rows, cols), BF16),
            pltpu.VMEM((ns, part, cols), F32),
            pltpu.VMEM((STEPS, nx, part, cols), F32),
            pltpu.VMEM((nx - 1, part, cols), F32),
            pltpu.VMEM((STEPS, nx - 1, part, cols), F32),
            pltpu.VMEM((part, cols), F32),
            pltpu.VMEM((n, 8, cols), F32),
            pltpu.VMEM((STEPS, n, 8, cols), F32),
            pltpu.VMEM((STEPS, n, 8, cols), F32),
            pltpu.VMEM((STEPS, ns, 8, cols), F32),
            pltpu.VMEM((STEPS, n, 8, cols), F32),
            pltpu.VMEM((STEPS, ns, 8, cols), F32),
            pltpu.VMEM((STEPS, ns, 8, cols), F32),
            pltpu.VMEM((STEPS, n, 8, cols), F32),
            dma((n,)),
            dma((2, n - 1)),
            dma((STEPS, 2, n - 1)),
            dma((STEPS, 2, n - 1)),
            dma((STEPS, 2, ns - 1)),
            dma((STEPS, 2, n - 1)),
            dma((STEPS, 2, ns - 1)),
            dma((STEPS, 2, ns - 1)),
            dma((STEPS, 2, n - 1)),
            dma((STEPS, 2, nz)),
            dma((STEPS, 2, nz - 1)),
            dma((STEPS, 2, nz - 1)),
            dma((STEPS, 2, nz)),
            dma((STEPS, 2, nx)),
            dma((STEPS, 2, nx - 1)),
            dma((STEPS, 2, nx - 1)),
            dma((STEPS, 2, nx)),
        ],
        compiler_params=pltpu.CompilerParams(
            collective_id=0, has_side_effects=True, vmem_limit_bytes=LIMIT
        ),
    )(idiosyncratic, factors, loadings, bars, given, eligible, holdings)


def on_device(
    factors, idiosyncratic, loadings, rating, barrier, loss_given, sector, allowed, holdings
):
    obl_dev = idiosyncratic.shape[0]
    scn_dev = idiosyncratic.shape[1]
    n = lax.axis_size("obl")
    ns = lax.axis_size("scn")
    obligors = obl_dev * n
    scenarios = scn_dev * ns
    tail_scale = 1.0 / ((1.0 - LEVEL) * scenarios)
    sector_hot = (sector[:, None] == jnp.arange(allowed.shape[1])[None, :]).astype(jnp.float32)
    eligible = lax.dot_general(
        sector_hot,
        allowed.astype(jnp.float32),
        (((1,), (1,)), ((), ())),
        precision=lax.Precision.HIGHEST,
    )
    rating_hot = (rating[:, None] == jnp.arange(barrier.shape[0])[None, :]).astype(jnp.float32)
    barrier_rows = jnp.dot(rating_hot, barrier, precision=lax.Precision.HIGHEST)
    out, short = descend(
        idiosyncratic, factors, loadings, barrier_rows[:, None], loss_given[:, None],
        eligible, holdings, n, ns, obligors, scenarios, tail_scale,
    )
    return (out.reshape(obl_dev, -1), short[:, 0, :])


def solution(mesh):
    return jax.shard_map(
        on_device,
        mesh=mesh,
        in_specs=(
            P("scn", None),
            P("obl", "scn"),
            P("obl", None),
            P("obl"),
            P(),
            P("obl"),
            P("obl"),
            P(),
            P("obl", None),
        ),
        out_specs=(P("obl", None), P()),
        check_vma=False,
    )
```

```python
import functools

import jax
import jax.numpy as jnp
from jax import lax
from jax.experimental import pallas as pl
from jax.experimental.pallas import tpu as pltpu
from jax.sharding import PartitionSpec as P

STEPS = 2


IDIO_SCALE = 0.8
SHARP = 2.0
LEVEL = 0.99
QUANTILE = 2.326
SMOOTH = 0.5
EPSILON = 1e-06
STEP_RATE = 8.0

MESH = pl.DeviceIdType.MESH
VMEM = pl.BlockSpec(memory_space=pltpu.VMEM)
LIMIT = 60 * 1024 * 1024
F32 = jnp.float32
BF16 = jnp.bfloat16


def push(src, dst, send, recv, axis, peer):
    return pltpu.make_async_remote_copy(
        src_ref=src,
        dst_ref=dst,
        send_sem=send,
        recv_sem=recv,
        device_id={axis: peer},
        device_id_type=MESH,
    )


def greet(groups):
    barrier = pltpu.get_barrier_semaphore()
    total = 0
    for axis, rank, size in groups:
        for step in range(1, size):
            pl.semaphore_signal(
                barrier, inc=1, device_id={axis: lax.rem(rank + step, size)}, device_id_type=MESH
            )
        total += size - 1
    pl.semaphore_wait(barrier, total)


def spread_out(buf, send, recv, axis, rank, size):
    copies = []
    for step in range(1, size):
        copy = push(
            buf.at[rank], buf.at[rank], send.at[step - 1], recv.at[step - 1], axis, lax.rem(rank + step, size)
        )
        copy.start()
        copies.append(copy)
    return copies


def wait_all(copies):
    for copy in copies:
        copy.wait()


def kernel(
    n, ns, obligors, scenarios, tail_scale,
    idio_ref, fact_ref, load_ref, bar_row, given_row, elig_ref, hold_ref,
    out_ref, short_ref,
    prob, expo, acc, away, near, far_out, far_in, losses, weight,
    grad, grad_near, grad_out, grad_in, pos,
    tot_buf, off_buf, sum_buf, scn_buf, tail_buf, tail_scn, new_scn, new_obl,
    bar_ref, given_ref, mean_out, mean_in,
    load_sem, tot_sem, mean_sem,
    off_sem, sum_sem, scn_sem, tail_sem, tsc_sem, nsc_sem, nob_sem,
    a_sem, b_sem, c_sem, d_sem, ga_sem, gb_sem, gc_sem, gd_sem,
):
    obl = lax.axis_index("obl")
    scn = lax.axis_index("scn")
    outer, inner = obl // 2, lax.rem(obl, 2)
    nz = n // 2
    mate = outer * 2 + 1 - inner
    souter, sinner = scn // 2, lax.rem(scn, 2)
    nx = ns // 2
    smate = souter * 2 + 1 - sinner
    obl_dev, cols = hold_ref.shape
    scn_dev = fact_ref.shape[0]
    rows = scn_dev // n
    part = obl_dev // ns
    targets = [lax.rem(outer + 1 + i, nz) for i in range(nz)]
    mates = [t * 2 + 1 - inner for t in targets]
    owns = [t * 2 + inner for t in targets]
    stargets = [lax.rem(souter + 1 + i, nx) for i in range(nx)]
    order = [p for pair in zip(mates, owns) for p in pair]

    loads = {}
    for where, piece in enumerate(order):
        copy = pltpu.make_async_copy(
            idio_ref.at[:, pl.ds(pl.multiple_of(piece * rows, 128), rows)], prob.at[piece], load_sem.at[where]
        )
        copy.start()
        loads[where] = copy
    total = jnp.zeros((1, cols), F32)
    for k in range(ns):
        span = pl.ds(k * part, part)
        total += jnp.sum(elig_ref[span, :] * hold_ref[span, :], axis=0, keepdims=True)
    tot_buf[obl] = jnp.broadcast_to(total, (8, cols))
    greet([("obl", obl, n), ("scn", scn, ns)])
    totals = spread_out(tot_buf, tot_sem.at[0], tot_sem.at[1], "obl", obl, n)
    tile = min(256, part)

    @pl.loop(0, obl_dev // 128)
    def _(t):
        span = pl.ds(pl.multiple_of(t * 128, 128), 128)
        bar_ref[span, :] = jnp.transpose(jnp.broadcast_to(bar_row[0:1, span], (128, 128)))
        given_ref[span, :] = jnp.transpose(jnp.broadcast_to(given_row[0:1, span], (128, 128)))


    def probabilities(where):
        piece = order[where]
        loads[where].wait()
        fact = fact_ref[pl.ds(pl.multiple_of(piece * rows, 128), rows), :]

        @pl.loop(0, obl_dev // tile)
        def _(t):
            span = pl.ds(pl.multiple_of(t * tile, tile), tile)
            latent = lax.dot_general(
                load_ref[span, :], fact, (((1,), (1,)), ((), ())), preferred_element_type=F32
            )
            latent = latent + IDIO_SCALE * prob[piece, span, :].astype(F32)
            half = 0.5 * jnp.tanh((latent - bar_ref[span, 0:1]) * (0.5 * SHARP))
            prob[piece, span, :] = (0.5 + half).astype(BF16)

    def partial_losses(step, piece):
        acc[...] = jnp.zeros_like(acc)

        @pl.loop(0, ns)
        def _(k):
            span = pl.ds(pl.multiple_of(k * part, part), part)
            acc[...] += jnp.dot(expo[step, k], prob[piece, span, :], preferred_element_type=F32)

    def add_gradient(piece, k, weights, fresh):
        span = pl.ds(pl.multiple_of(k * part, part), part)
        value = jnp.dot(prob[piece, span, :], weights, preferred_element_type=F32)
        if fresh:
            grad[k] = value
        else:
            grad[k] += value

    def add_piece(step, piece, fresh=False):
        weights = weight[step, piece]

        @pl.loop(0, ns)
        def _(k):
            add_gradient(piece, k, weights, fresh)

    probabilities(0)
    wait_all(totals)
    total = jnp.sum(tot_buf[...], axis=0)[0:1, :]
    for k in range(ns):
        span = pl.ds(k * part, part)
        start = obligors * (elig_ref[span, :] * hold_ref[span, :]) / total
        expo[0, k] = jnp.transpose(given_ref[span, 0:1] * start / obligors).astype(BF16)
    mine = pl.ds(pl.multiple_of(scn * part, part), part)
    pos[...] = obligors * (elig_ref[mine, :] * hold_ref[mine, :]) / total
    row = lax.broadcasted_iota(jnp.int32, (8, cols), 0)

    for step in range(STEPS):
        last = step == STEPS - 1
        pair, line = [], []
        offset = None

        def send_mate(i):
            nonlocal offset
            if step == 0 and i > 0:
                probabilities(2 * i)
            partial_losses(step, mates[i])
            if step > 0:
                acc[...] *= inverse
            if i == 0:
                offset = jnp.sum(acc[...], axis=1, keepdims=True) * (1.0 / rows)
                off_buf[step, obl] = jnp.transpose(jnp.broadcast_to(offset, (cols, 128)))[0:8, :]
            away[i] = (acc[...] - offset).astype(BF16)
            copy = push(away.at[i], near.at[step, i], a_sem.at[step, 0, i], a_sem.at[step, 1, i], "obl", mate)
            copy.start()
            pair.append(copy)

        send_mate(0)
        offsets = spread_out(off_buf.at[step], off_sem.at[step, 0], off_sem.at[step, 1], "obl", obl, n)
        send_mate(1)
        for i in range(nz):
            if step == 0:
                probabilities(2 * i + 1)
            partial_losses(step, owns[i])
            if step > 0:
                acc[...] *= inverse
            pair[i].wait_recv()
            value = acc[...] - offset + near[step, i].astype(F32)
            if i < nz - 1:
                far_out[i] = value.astype(BF16)
                copy = push(
                    far_out.at[i], far_in.at[step, i], b_sem.at[step, 0, i], b_sem.at[step, 1, i], "obl", owns[i]
                )
                copy.start()
                line.append(copy)
            else:
                losses[...] = value
            if i + 2 < nz:
                send_mate(i + 2)
        wait_all(offsets)
        for i in range(nz - 1):
            line[i].wait_recv()
            losses[...] += far_in[step, i].astype(F32)
        value = jnp.transpose(losses[...])
        first = jnp.sum(value, axis=0, keepdims=True)
        second = jnp.sum(value * value, axis=0, keepdims=True)
        sum_buf[step, obl] = jnp.where(row == 0, first, second)
        wait_all(spread_out(sum_buf.at[step], sum_sem.at[step, 0], sum_sem.at[step, 1], "obl", obl, n))
        base = jnp.sum(off_buf[step], axis=0)
        scn_buf[step, scn] = jnp.where(row == 2, base, jnp.sum(sum_buf[step], axis=0))
        wait_all(spread_out(scn_buf.at[step], scn_sem.at[step, 0], scn_sem.at[step, 1], "scn", scn, ns))
        center = jnp.zeros((1, cols), F32)
        for k in range(ns):
            center += scn_buf[step, k, 0:1, :] + scn_dev * scn_buf[step, k, 2:3, :]
        center = center / scenarios
        spread = jnp.zeros((1, cols), F32)
        for k in range(ns):
            gap = scn_buf[step, k, 2:3, :] - center
            spread += scn_buf[step, k, 1:2, :] + 2.0 * gap * scn_buf[step, k, 0:1, :] + scn_dev * (gap * gap)
        spread = spread / scenarios
        deviation = jnp.sqrt(spread + EPSILON)
        thresh = center + QUANTILE * deviation
        width = SMOOTH * deviation
        scaled = (jnp.transpose(losses[...]) + (base[0:1, :] - thresh)) / width
        weight[step, obl] = (jax.nn.sigmoid(scaled) * tail_scale).astype(BF16)

        def give(slot, index, sems, axis, peer):
            ref = weight.at[step, slot]
            copy = push(ref, ref, sems.at[step, 0, index], sems.at[step, 1, index], axis, peer)
            copy.start()
            return copy

        own = give(obl, nz - 1, d_sem, "obl", mate)
        gather = [give(obl, i, c_sem, "obl", owns[i]) for i in range(nz - 1)]
        soft = jnp.maximum(scaled, 0.0) + jnp.log1p(jnp.exp(-jnp.abs(scaled)))
        tail_buf[step, obl] = jnp.broadcast_to(jnp.sum(soft, axis=0, keepdims=True), (8, cols))
        tails = spread_out(tail_buf.at[step], tail_sem.at[step, 0], tail_sem.at[step, 1], "obl", obl, n)
        add_piece(step, obl, fresh=True)
        own.wait_recv()
        add_piece(step, mate)
        passed = []
        sources = [lax.rem(outer + nz - 1 - i, nz) for i in range(nz - 1)]
        for i in range(nz - 1):
            gather[i].wait_recv()
            slot = sources[i] * 2 + inner
            passed.append(give(slot, i, d_sem, "obl", mate))
            add_piece(step, slot)
        wait_all(tails)
        tail_scn[step, scn] = jnp.sum(tail_buf[step], axis=0)
        scn_tails = spread_out(tail_scn.at[step], tsc_sem.at[step, 0], tsc_sem.at[step, 1], "scn", scn, ns)
        for i in range(nz - 2):
            passed[i].wait_recv()
            add_piece(step, sources[i] * 2 + 1 - inner)
        passed[nz - 2].wait_recv()
        final = sources[nz - 2] * 2 + 1 - inner
        final_weights = weight[step, final]

        gpair, gline, gmean = [], [], []
        for i in range(nx):
            slot = stargets[i] * 2 + 1 - sinner
            add_gradient(final, slot, final_weights, False)
            copy = push(
                grad.at[slot], grad_near.at[step, i], ga_sem.at[step, 0, i], ga_sem.at[step, 1, i], "scn", smate
            )
            copy.start()
            gpair.append(copy)
        for i in range(nx):
            slot = stargets[i] * 2 + sinner
            add_gradient(final, slot, final_weights, False)
            gpair[i].wait_recv()
            if i < nx - 1:
                value = grad[slot] + grad_near[step, i]
                mean = jnp.sum(value, axis=1, keepdims=True) * (1.0 / cols)
                mean_out[i] = jnp.transpose(jnp.broadcast_to(mean, (part, 128)))[0:8, :]
                grad_out[i] = (value - mean).astype(BF16)
                copy = push(
                    mean_out.at[i], mean_in.at[step, i], mean_sem.at[step, 0, i], mean_sem.at[step, 1, i], "scn", slot
                )
                copy.start()
                gmean.append(copy)
                copy = push(
                    grad_out.at[i], grad_in.at[step, i], gb_sem.at[step, 0, i], gb_sem.at[step, 1, i], "scn", slot
                )
                copy.start()
                gline.append(copy)
        wait_all(scn_tails)
        short_ref[step] = thresh + width * (jnp.sum(tail_scn[step], axis=0) * tail_scale)
        gradient = grad[scn] + grad_near[step, nx - 1]
        for i in range(nx - 1):
            gline[i].wait_recv()
            gmean[i].wait_recv()
            mean = jnp.transpose(jnp.broadcast_to(mean_in[step, i, 0:1, :], (128, part)))[:, 0:1]
            gradient += grad_in[step, i].astype(F32) + mean
        gradient = given_ref[mine, 0:1] * elig_ref[mine, :] * gradient
        unnorm = pos[...] * jnp.exp(-STEP_RATE * gradient)
        pos[...] = unnorm
        if last:
            out_ref[scn] = unnorm
        else:
            expo[step + 1, scn] = jnp.transpose(given_ref[mine, 0:1] * unnorm).astype(BF16)

        def hand(slot, index, sems, peer):
            ref = out_ref.at[slot] if last else expo.at[step + 1, slot]
            copy = push(ref, ref, sems.at[step, 0, index], sems.at[step, 1, index], "scn", peer)
            copy.start()
            return copy

        mine_copy = hand(scn, nx - 1, gd_sem, smate)
        ggather = [hand(scn, i, gc_sem, stargets[i] * 2 + sinner) for i in range(nx - 1)]
        new_scn[step, scn] = jnp.broadcast_to(jnp.sum(unnorm, axis=0, keepdims=True), (8, cols))
        new_totals = spread_out(new_scn.at[step], nsc_sem.at[step, 0], nsc_sem.at[step, 1], "scn", scn, ns)
        gpassed = [mine_copy]
        for i in range(nx - 1):
            ggather[i].wait_recv()
            slot = lax.rem(souter + nx - 1 - i, nx) * 2 + sinner
            gpassed.append(hand(slot, i, gd_sem, smate))
        wait_all(new_totals)
        new_obl[step, obl] = jnp.sum(new_scn[step], axis=0)
        new_totals = spread_out(new_obl.at[step], nob_sem.at[step, 0], nob_sem.at[step, 1], "obl", obl, n)
        for copy in gpassed:
            copy.wait_recv()
        wait_all(new_totals)
        total = jnp.sum(new_obl[step], axis=0)[0:1, :]
        own.wait_send()
        for copy in pair + line + gather + passed + gpair + gline + gmean + ggather + gpassed:
            copy.wait_send()
        if last:
            for k in range(ns):
                out_ref[k] = obligors * out_ref[k] / total
        else:
            pos[...] = obligors * pos[...] / total
            inverse = jnp.transpose(jnp.broadcast_to(1.0 / total, (128, cols)))[:, 0:1]


def descend(idiosyncratic, factors, loadings, bars, given, eligible, holdings, n, ns, obligors, scenarios, tail_scale):
    obl_dev, cols = holdings.shape
    scn_dev = factors.shape[0]
    rows, part = scn_dev // n, obl_dev // ns
    nz, nx = n // 2, ns // 2
    dma = pltpu.SemaphoreType.DMA
    return pl.pallas_call(
        functools.partial(kernel, n, ns, obligors, scenarios, tail_scale),
        out_shape=(
            jax.ShapeDtypeStruct((ns, part, cols), F32),
            jax.ShapeDtypeStruct((STEPS, 8, cols), F32),
        ),
        in_specs=[pl.BlockSpec(memory_space=pl.ANY)] + [VMEM] * 6,
        out_specs=(VMEM, VMEM),
        scratch_shapes=[
            pltpu.VMEM((n, obl_dev, rows), BF16),
            pltpu.VMEM((STEPS, ns, cols, part), BF16),
            pltpu.VMEM((cols, rows), F32),
            pltpu.VMEM((nz, cols, rows), BF16),
            pltpu.VMEM((STEPS, nz, cols, rows), BF16),
            pltpu.VMEM((nz - 1, cols, rows), BF16),
            pltpu.VMEM((STEPS, nz - 1, cols, rows), BF16),
            pltpu.VMEM((cols, rows), F32),
            pltpu.VMEM((STEPS, n, rows, cols), BF16),
            pltpu.VMEM((ns, part, cols), F32),
            pltpu.VMEM((STEPS, nx, part, cols), F32),
            pltpu.VMEM((nx - 1, part, cols), BF16),
            pltpu.VMEM((STEPS, nx - 1, part, cols), BF16),
            pltpu.VMEM((part, cols), F32),
            pltpu.VMEM((n, 8, cols), F32),
            pltpu.VMEM((STEPS, n, 8, cols), F32),
            pltpu.VMEM((STEPS, n, 8, cols), F32),
            pltpu.VMEM((STEPS, ns, 8, cols), F32),
            pltpu.VMEM((STEPS, n, 8, cols), F32),
            pltpu.VMEM((STEPS, ns, 8, cols), F32),
            pltpu.VMEM((STEPS, ns, 8, cols), F32),
            pltpu.VMEM((STEPS, n, 8, cols), F32),
            pltpu.VMEM((obl_dev, 128), F32),
            pltpu.VMEM((obl_dev, 128), F32),
            pltpu.VMEM((nx - 1, 8, part), F32),
            pltpu.VMEM((STEPS, nx - 1, 8, part), F32),
            dma((n,)),
            dma((2, n - 1)),
            dma((STEPS, 2, nx - 1)),
            dma((STEPS, 2, n - 1)),
            dma((STEPS, 2, n - 1)),
            dma((STEPS, 2, ns - 1)),
            dma((STEPS, 2, n - 1)),
            dma((STEPS, 2, ns - 1)),
            dma((STEPS, 2, ns - 1)),
            dma((STEPS, 2, n - 1)),
            dma((STEPS, 2, nz)),
            dma((STEPS, 2, nz - 1)),
            dma((STEPS, 2, nz - 1)),
            dma((STEPS, 2, nz)),
            dma((STEPS, 2, nx)),
            dma((STEPS, 2, nx - 1)),
            dma((STEPS, 2, nx - 1)),
            dma((STEPS, 2, nx)),
        ],
        compiler_params=pltpu.CompilerParams(
            collective_id=0, has_side_effects=True, vmem_limit_bytes=LIMIT
        ),
    )(idiosyncratic, factors, loadings, bars, given, eligible, holdings)


def on_device(
    factors, idiosyncratic, loadings, rating, barrier, loss_given, sector, allowed, holdings
):
    obl_dev = idiosyncratic.shape[0]
    scn_dev = idiosyncratic.shape[1]
    n = lax.axis_size("obl")
    ns = lax.axis_size("scn")
    obligors = obl_dev * n
    scenarios = scn_dev * ns
    tail_scale = 1.0 / ((1.0 - LEVEL) * scenarios)
    sector_hot = (sector[:, None] == jnp.arange(allowed.shape[1])[None, :]).astype(jnp.float32)
    eligible = lax.dot_general(
        sector_hot,
        allowed.astype(jnp.float32),
        (((1,), (1,)), ((), ())),
        precision=lax.Precision.HIGHEST,
    )
    rating_hot = (rating[:, None] == jnp.arange(barrier.shape[0])[None, :]).astype(jnp.float32)
    barrier_rows = jnp.dot(rating_hot, barrier, precision=lax.Precision.HIGHEST)
    out, short = descend(
        idiosyncratic, factors, loadings, barrier_rows[None, :], loss_given[None, :],
        eligible, holdings, n, ns, obligors, scenarios, tail_scale,
    )
    return (out.reshape(obl_dev, -1), short[:, 0, :])


def solution(mesh):
    return jax.shard_map(
        on_device,
        mesh=mesh,
        in_specs=(
            P("scn", None),
            P("obl", "scn"),
            P("obl", None),
            P("obl"),
            P(),
            P("obl"),
            P("obl"),
            P(),
            P("obl", None),
        ),
        out_specs=(P("obl", None), P()),
        check_vma=False,
    )
```
